32 devices in a mesh: req: 4 (over y, core), exp: 8 (over z, x).
Axes of the slice: x: 2, y: 2, z: 4, core: 2. Of those that a mesh axis runs over, the one named last changes fastest.
Arguments:
- queries: bfloat16 [8, 512, 2048], P('req', None, 'exp'), may hold values from -40 to 40
- new_entries: bfloat16 [8, 2, 512, 2048], P('req', None, None, 'exp'), may hold values from -40 to 40
- cache_entries: bfloat16 [8, 2, 4096, 2048], P('req', None, None, 'exp'), may hold values from -6 to 6
- cache_lengths: int32 [8], P('req'), may hold values from 1 to 4096, 16384 in all
- out_proj: bfloat16 [2048, 2048], P('exp'), may hold values from -0.125 to 0.125
- residual: bfloat16 [4096, 2048], P(('req', 'exp')), may hold values from -40 to 40
- norm_gain: float32 [2048], replicated, may hold values from 0.1 to 1.9
- routes: int32 [4096, 8], P(('req', 'exp')), may hold values from 0 to 63, all different within a row; in each aligned block of 128 rows (0 to 127, 128 to 255, ...) at most 20 rows name the same one
- gate_weights: float32 [4096, 8], P(('req', 'exp')), may hold values from 0.1 to 0.6
- expert_in: bfloat16 [2, 2048, 65536], P(None, None, ('req', 'exp')), may hold values from -0.125 to 0.125
- expert_down: bfloat16 [65536, 2048], P(('req', 'exp')), may hold values from -0.1875 to 0.1875
Outputs:
- attended: bfloat16 [4096, 2048], P(('req', 'exp'))
- expert_out: bfloat16 [4096, 2048], P(('req', 'exp'))
The draws below stay inside these ranges and needn't reach their ends.
Inputs may be any that keep to these rules, and one draw needn't show every extreme that they name: `cache_lengths`: the lengths add up to 16384 and one is exactly 4096. `routes`: each row names 8 different experts; within the rows of one device (aligned blocks of 128 rows) no expert is named more than 20 times, a bound that some block reaches.
All inputs are finite; a program needn't handle non-finite values. No bound on the sum of `cache_lengths` on one device may be relied on, other than what follows from the above.
Results may differ from the reference program's by a relative error of at most 0.0085.
Values may be sent and summed in bfloat16 or wider, within the bound.
A program may use at most 128 MiB of HBM per device.

```python
import math
import jax
import jax.numpy as jnp
import numpy as np
from jax import lax

D = 2048
HEADS = 16
HD = 128
EXPERTS = 64
FF = 1024
TOP = 8
NEW = 512
CACHE = 4096
REQUESTS = 8
TOKENS = 4096
TOK_DEV = 128
CAP = 20


def draw_queries(key, part):
    shape = (REQUESTS, NEW, HEADS, HD)
    values = jax.random.normal(jax.random.fold_in(key, 1), shape, jnp.float32)
    return values.reshape(REQUESTS, NEW, HEADS * HD).astype(jnp.bfloat16)


def draw_new_entries(key, part):
    shape = (REQUESTS, 2, NEW, HEADS, HD)
    values = jax.random.normal(jax.random.fold_in(key, 2), shape, jnp.float32)
    return values.reshape(REQUESTS, 2, NEW, HEADS * HD).astype(jnp.bfloat16)


def draw_residual(key, part):
    base = jnp.clip(jax.random.normal(jax.random.fold_in(key, 3), (TOKENS, D), jnp.float32), -4.0, 4.0)
    row_scale = jnp.exp(jax.random.uniform(jax.random.fold_in(key, 4), (TOKENS, 1), jnp.float32, math.log(0.3), math.log(3.0)))
    col_scale = jnp.exp(jax.random.uniform(jax.random.fold_in(key, 5), (1, D), jnp.float32, math.log(0.3), math.log(3.0)))
    return (base * row_scale * col_scale).astype(jnp.bfloat16)


def levels(rng, extent, pieces, smallest, high):
    gain, own = 1.0, jax.random.fold_in(rng, 6)
    for position, shards_of in pieces:
        steps = jnp.exp(jax.random.uniform(jax.random.fold_in(own, position), (shards_of,), jnp.float32, smallest / len(pieces), high / len(pieces)))
        gain = gain * jnp.repeat(steps, extent[position] // shards_of).reshape([-1 if axis == position else 1 for axis in range(len(extent))])
    return gain


def split_up(amount, total, limit, lean):
    loads = [(1 << 20) // math.isqrt(standing ** lean) + 1 for standing in range(2, amount + 1)]
    surplus, counts = total - limit - (amount - 1), [1] * (amount - 1)
    while surplus > 0:
        candidates = [i for i in range(amount - 1) if counts[i] < limit]
        pool, remaining = sum([loads[i] for i in candidates]), surplus
        for i in candidates:
            addition = min(limit - counts[i], max(1, remaining * loads[i] // pool), surplus)
            counts[i] = counts[i] + addition
            surplus = surplus - addition
    return np.array([limit] + counts)


def uneven(stream_key, number_of, total, reach, skew):
    if number_of == 2:
        one = jax.random.randint(stream_key, (), max(1, total - reach), min(reach, total - 1) + 1)
        return jnp.stack([one, total - one])
    tallies = jnp.asarray(split_up(number_of, total, reach, skew), jnp.int32)
    twos = (number_of - 1) // 2
    giver, sink = tallies[1:1 + 2 * twos:2], tallies[2:2 + 2 * twos:2]
    slack = jnp.minimum(giver - 1, reach - sink)
    passed = jax.random.randint(jax.random.fold_in(stream_key, 1), (twos,), 0, 1 << 20) % (slack + 1)
    tallies = tallies.at[1:1 + 2 * twos:2].set(giver - passed).at[2:2 + 2 * twos:2].set(sink + passed)
    return tallies[jax.random.permutation(jax.random.fold_in(stream_key, 2), number_of)]


def shared_out(key, own, number, rows, amount, top, reach, slope):
    order = jax.random.permutation(key, amount)
    crowded, common = shares(amount, rows * top, reach, slope, True), shares(amount, rows * top, reach, slope, False)
    places = jnp.arange(amount)

    def named(sizes, rotation):
        used = int((sizes > 0).sum())
        fixed = max(1, used // 4)
        shifted = fixed + (places - fixed + rotation * (used - fixed)) % max(1, amount - fixed)
        return jnp.zeros((amount,), jnp.int32).at[order[jnp.where(places < fixed, places, shifted)]].set(jnp.asarray(sizes, jnp.int32))

    sizes = jnp.where(number % 4 == 0, named(crowded, number // 4), named(common, number - number // 4 - 1))
    mixed = jax.random.permutation(jax.random.fold_in(own, 3), amount)
    source_of, taker = mixed[0:amount // 2 * 2:2], mixed[1:amount // 2 * 2:2]
    slack = jnp.minimum(sizes[source_of] - 1, reach - sizes[taker]) // 2
    slack = jnp.where((source_of == order[0]) | (taker == order[0]) | (sizes[taker] == 0), 0, jnp.maximum(slack, 0))
    shifted = jax.random.randint(jax.random.fold_in(own, 4), (amount // 2,), 0, 1 << 20) % (slack + 1)
    sizes = sizes.at[source_of].add(-shifted).at[taker].add(shifted)
    members = jnp.searchsorted(jnp.cumsum(sizes), jnp.arange(rows * top), side="right").astype(jnp.int32)
    table = members.reshape(top, rows).T
    table = table[jax.random.permutation(jax.random.fold_in(own, 1), rows)]
    rotation = jax.random.randint(jax.random.fold_in(own, 2), (rows, 1), 0, top)
    return jnp.take_along_axis(table, (jnp.arange(top)[None, :] + rotation) % top, axis=1)


def shares(count, total, most, slope, full):
    loads = [(1 << 20) // math.isqrt(standing ** slope) + 1 for standing in range(1, count + 1)]
    largest = most if full else min(most, max(-(-total // count), total * loads[0] // sum(loads)))
    least = 1 if total - largest >= count - 1 else 0
    counts, rest = [largest] + [least] * (count - 1), total - largest - least * (count - 1)
    while rest > 0:
        free = [i for i in range(1, count) if counts[i] < largest] or [i for i in range(1, count) if counts[i] < most]
        whole, budget = sum([loads[i] for i in free]), rest
        for i in free:
            addition = min(most - counts[i], max(1, budget * loads[i] // whole), rest)
            counts[i] = counts[i] + addition
            rest = rest - addition
    return np.array(counts)


def normal_values(key, dims, deviation, most, split=(), kind=jnp.bfloat16):
    factor_of = levels(key, dims, split, -0.22, 0.18) if split else 1.0
    values = jax.random.normal(key, dims, jnp.float32) * deviation * factor_of
    return jnp.minimum(jnp.maximum(values, -most), most).astype(kind)


def setup_inputs(seed: int = 0) -> dict:
    key_list = jax.random.split(jax.random.key(seed), 12)
    queries = draw_queries(jax.random.fold_in(key_list[11], 71), 0)
    new_entries = draw_new_entries(jax.random.fold_in(key_list[11], 71), 0)
    cache_entries = normal_values(key_list[2], (REQUESTS, 2, CACHE, HEADS * HD), 1.0, 6.0, ((0, 4), (3, 8)))
    cache_lengths = uneven(key_list[3], REQUESTS, REQUESTS * CACHE // 2, CACHE, 2).astype(jnp.int32)
    out_proj = normal_values(key_list[4], (HEADS * HD, D), (HEADS * HD) ** -0.5, 0.125, ((0, 8),))
    residual = draw_residual(jax.random.fold_in(key_list[11], 71), 0)
    norm_gain = jnp.clip(1.0 + 0.18 * jax.random.normal(key_list[6], (D,), jnp.float32), 0.1, 1.9)
    routes_keys = jax.random.split(jax.random.fold_in(key_list[7], 1), TOKENS // TOK_DEV)
    routes_turns = jax.random.permutation(jax.random.fold_in(key_list[7], 3), TOKENS // TOK_DEV)
    routes = jax.vmap(lambda own, number: shared_out(jax.random.fold_in(key_list[7], 2), own, number, TOK_DEV, EXPERTS, TOP, CAP, 2))(routes_keys, routes_turns).reshape((TOKENS, TOP))
    gate_weights = jnp.clip(0.1 + 0.5 * jax.random.uniform(key_list[8], (TOKENS, TOP), jnp.float32) ** levels(key_list[8], (TOKENS, TOP), ((0, 32),), -0.2, 0.2), 0.1, 0.6)
    expert_in = normal_values(key_list[9], (2, D, EXPERTS * FF), D ** -0.5, 0.125, ((2, 32),))
    expert_down = normal_values(key_list[10], (EXPERTS * FF, D), FF ** -0.5, 0.1875, ((0, 32),))
    return dict(queries=queries, new_entries=new_entries, cache_entries=cache_entries, cache_lengths=cache_lengths, out_proj=out_proj, residual=residual, norm_gain=norm_gain, routes=routes, gate_weights=gate_weights, expert_in=expert_in, expert_down=expert_down)


def attend_request(packed):
    query_rows, new_rows, cache_rows, length = packed
    query_heads = query_rows.astype(jnp.float32).reshape(NEW, HEADS, HD)
    cache_keys = cache_rows[0].astype(jnp.float32).reshape(CACHE, HEADS, HD)
    cache_vals = cache_rows[1].astype(jnp.float32).reshape(CACHE, HEADS, HD)
    new_keys = new_rows[0].astype(jnp.float32).reshape(NEW, HEADS, HD)
    new_vals = new_rows[1].astype(jnp.float32).reshape(NEW, HEADS, HD)
    scale = HD ** (-0.5)
    cache_scores = jnp.einsum('thd,jhd->htj', query_heads, cache_keys) * scale
    new_scores = jnp.einsum('thd,jhd->htj', query_heads, new_keys) * scale
    cache_valid = jnp.arange(CACHE, dtype=jnp.int32) < length
    causal = jnp.arange(NEW, dtype=jnp.int32)[None, :] <= jnp.arange(NEW, dtype=jnp.int32)[:, None]
    scores = jnp.concatenate([jnp.where(cache_valid[None, None, :], cache_scores, -1e+30), jnp.where(causal[None, :, :], new_scores, -1e+30)], axis=-1)
    peak = lax.optimization_barrier(jnp.max(scores, axis=-1, keepdims=True))
    weights = jnp.exp(scores - peak)
    denoms = lax.optimization_barrier(jnp.sum(weights, axis=-1))
    weights_bf = lax.optimization_barrier(weights.astype(jnp.bfloat16)).astype(jnp.float32)
    all_vals = jnp.concatenate([cache_vals, new_vals], axis=0)
    mixed = jnp.einsum('htj,jhd->thd', weights_bf, all_vals) / jnp.transpose(denoms)[:, :, None]
    return mixed.astype(jnp.bfloat16).reshape(NEW, HEADS * HD)

def reference(queries, new_entries, cache_entries, cache_lengths, out_proj, residual, norm_gain, routes, gate_weights, expert_in, expert_down):
    attention = lax.map(attend_request, (queries, new_entries, cache_entries, cache_lengths))
    attention = attention.reshape(TOKENS, HEADS * HD)
    hidden = residual.astype(jnp.float32) + jnp.dot(attention, out_proj, preferred_element_type=jnp.float32)
    attended = hidden.astype(jnp.bfloat16)
    mean_square = lax.optimization_barrier(jnp.mean(hidden * hidden, axis=-1, keepdims=True))
    normed = (hidden * lax.rsqrt(mean_square + 1e-05) * norm_gain).astype(jnp.bfloat16)
    assign_total = TOKENS * TOP
    blocks = TOKENS // TOK_DEV
    flat_routes = routes.reshape(assign_total).astype(jnp.int32)
    onehot = (flat_routes[:, None] == jnp.arange(EXPERTS, dtype=jnp.int32)[None, :]).astype(jnp.int32)
    onehot = onehot.reshape(blocks, TOK_DEV * TOP, EXPERTS)
    slot_index = (lax.optimization_barrier(jnp.sum(jnp.cumsum(onehot, axis=1) * onehot, axis=2)) - 1).reshape(assign_total)
    block_index = jnp.arange(assign_total, dtype=jnp.int32) // (TOK_DEV * TOP)
    positions = (block_index * CAP + slot_index).astype(jnp.int32)
    token_index = jnp.arange(assign_total, dtype=jnp.int32) // TOP
    flat_gates = gate_weights.reshape(assign_total)
    padded = jnp.concatenate([normed, jnp.zeros((1, D), jnp.bfloat16)], axis=0)
    slots_total = blocks * CAP
    half_units = FF // 2

    def one_expert(running, expert):
        chosen = flat_routes == expert
        target = jnp.where(chosen, positions, slots_total).astype(jnp.int32)
        rows_table = jnp.full((slots_total,), TOKENS, jnp.int32).at[target].set(token_index, mode='drop')
        gate_table = jnp.zeros((slots_total,), jnp.float32).at[target].set(flat_gates, mode='drop')
        rows = padded[rows_table]
        weights_in = lax.dynamic_slice_in_dim(expert_in, expert * FF, FF, 2)
        weights_down = lax.dynamic_slice_in_dim(expert_down, expert * FF, FF, 0)
        gate_part = jnp.dot(rows, weights_in[0], preferred_element_type=jnp.float32)
        up_part = jnp.dot(rows, weights_in[1], preferred_element_type=jnp.float32)
        inner = (jax.nn.silu(gate_part) * up_part).astype(jnp.bfloat16)
        first = jnp.dot(inner[:, :half_units], weights_down[:half_units], preferred_element_type=jnp.float32).astype(jnp.bfloat16)
        second = jnp.dot(inner[:, half_units:], weights_down[half_units:], preferred_element_type=jnp.float32).astype(jnp.bfloat16)
        combined = lax.optimization_barrier(first).astype(jnp.float32) + lax.optimization_barrier(second).astype(jnp.float32)
        running = running.at[rows_table].add(gate_table[:, None] * combined, mode='drop')
        return (running, None)
    totals, _ = lax.scan(one_expert, jnp.zeros((TOKENS, D), jnp.float32), jnp.arange(EXPERTS, dtype=jnp.int32))
    return (attended, totals.astype(jnp.bfloat16))
```

```python
import jax
import jax.numpy as jnp
from jax import lax
from jax.sharding import PartitionSpec as P

HD = 128
EXPERTS = 64
FF = 1024
TOP = 8


def local(
    queries,
    new_entries,
    cache_entries,
    cache_lengths,
    out_proj,
    residual,
    norm_gain,
    routes,
    gate_weights,
    expert_in,
    expert_down,
):
    req_local, new_len, width_local = queries.shape
    heads_local = width_local // HD
    cache_len = cache_entries.shape[2]
    tok_local = residual.shape[0]
    model_width = residual.shape[1]

    full_proj = lax.all_gather(out_proj, "exp", axis=0, tiled=True)

    def attend_request(packed):
        query_rows, new_rows, cache_rows, length = packed
        query_heads = query_rows.reshape(new_len, heads_local, HD)
        cache_keys = cache_rows[0].reshape(cache_len, heads_local, HD)
        cache_vals = cache_rows[1].reshape(cache_len, heads_local, HD)
        new_keys = new_rows[0].reshape(new_len, heads_local, HD)
        new_vals = new_rows[1].reshape(new_len, heads_local, HD)
        scale = HD ** (-0.5)
        cache_scores = (
            jnp.einsum("thd,jhd->htj", query_heads, cache_keys, preferred_element_type=jnp.float32)
            * scale
        )
        new_scores = (
            jnp.einsum("thd,jhd->htj", query_heads, new_keys, preferred_element_type=jnp.float32)
            * scale
        )
        cache_valid = jnp.arange(cache_len, dtype=jnp.int32) < length
        causal = (
            jnp.arange(new_len, dtype=jnp.int32)[None, :]
            <= jnp.arange(new_len, dtype=jnp.int32)[:, None]
        )
        scores = jnp.concatenate(
            [
                jnp.where(cache_valid[None, None, :], cache_scores, -1e30),
                jnp.where(causal[None, :, :], new_scores, -1e30),
            ],
            axis=-1,
        )
        peak = jnp.max(scores, axis=-1, keepdims=True)
        weights = jnp.exp(scores - peak)
        denoms = jnp.sum(weights, axis=-1)
        weights_bf = weights.astype(jnp.bfloat16)
        all_vals = jnp.concatenate([cache_vals, new_vals], axis=0)
        mixed = jnp.einsum("htj,jhd->thd", weights_bf, all_vals, preferred_element_type=jnp.float32)
        mixed = mixed / jnp.transpose(denoms)[:, :, None]
        return mixed.astype(jnp.bfloat16).reshape(new_len, width_local)

    attention = lax.map(attend_request, (queries, new_entries, cache_entries, cache_lengths))
    attention = attention.reshape(req_local * new_len, width_local)
    features = lax.all_to_all(attention, "exp", split_axis=0, concat_axis=1, tiled=True)
    projected = jnp.dot(features, full_proj, preferred_element_type=jnp.float32)
    hidden = residual.astype(jnp.float32) + projected
    attended = hidden.astype(jnp.bfloat16)
    mean_square = jnp.mean(hidden * hidden, axis=-1, keepdims=True)
    normed = (hidden * lax.rsqrt(mean_square + 1e-05) * norm_gain).astype(jnp.bfloat16)
    devices = lax.axis_size("req") * lax.axis_size("exp")
    width_units = expert_in.shape[2]
    copies = max(1, FF // width_units)
    experts_local = max(1, width_units // FF)
    capacity = max(2, tok_local * TOP * 5 // (EXPERTS * 4))
    slots = EXPERTS * copies * capacity
    onehot = routes[:, :, None] == jnp.arange(EXPERTS, dtype=jnp.int32)[None, None, :]
    chosen = jnp.any(onehot, axis=1).astype(jnp.bfloat16)
    token_ids = jnp.arange(tok_local, dtype=jnp.int32)
    earlier = (token_ids[None, :] < token_ids[:, None]).astype(jnp.bfloat16)
    rank = jnp.dot(earlier, chosen, preferred_element_type=jnp.float32).astype(jnp.int32)
    slot_index = jnp.sum(jnp.where(onehot, rank[:, None, :], 0), axis=2)
    positions = routes * capacity + slot_index
    slot_ids = jnp.arange(slots, dtype=jnp.int32)
    slot_keys = slot_ids // (copies * capacity) * capacity + slot_ids % capacity
    places = jnp.transpose(positions)
    fill = jnp.zeros((slots, tok_local), jnp.bool_)
    mix = jnp.zeros((tok_local, slots), jnp.float32)
    for choice in range(TOP):
        fill = fill | (slot_keys[:, None] == places[choice][None, :])
        mix = mix + jnp.where(
            positions[:, choice][:, None] == slot_keys[None, :],
            gate_weights[:, choice][:, None],
            0.0,
        )
    outgoing = jnp.dot(
        fill.astype(jnp.bfloat16), normed, preferred_element_type=jnp.float32
    ).astype(jnp.bfloat16)
    items = experts_local * capacity
    outgoing = outgoing.reshape(devices, items, model_width)
    arrived = lax.all_to_all(outgoing, ("req", "exp"), split_axis=0, concat_axis=0, tiled=True)
    rows = arrived.reshape(devices * items, model_width)
    gate_part = jnp.dot(rows, expert_in[0], preferred_element_type=jnp.float32)
    up_part = jnp.dot(rows, expert_in[1], preferred_element_type=jnp.float32)
    row_expert = jnp.arange(devices * items, dtype=jnp.int32) % items // capacity
    unit_expert = jnp.arange(width_units, dtype=jnp.int32) // FF
    own = row_expert[:, None] == unit_expert[None, :]
    inner = jnp.where(own, jax.nn.silu(gate_part) * up_part, 0.0).astype(jnp.bfloat16)
    outputs = jnp.dot(inner, expert_down, preferred_element_type=jnp.float32).astype(jnp.bfloat16)
    returned = lax.all_to_all(
        outputs.reshape(devices, items, model_width),
        ("req", "exp"),
        split_axis=0,
        concat_axis=0,
        tiled=True,
    ).reshape(slots, model_width)
    first = lax.reduce_precision(mix, 8, 7)
    second = lax.reduce_precision(mix - first, 8, 7)
    third = mix - first - second
    terms = jnp.concatenate([first, second, third], axis=0).astype(jnp.bfloat16)
    mixed = jnp.dot(terms, returned, preferred_element_type=jnp.float32)
    mixed = mixed.reshape(3, tok_local, model_width)
    expert_out = (mixed[0] + mixed[1] + mixed[2]).astype(jnp.bfloat16)
    return (attended, expert_out)


def solution(mesh):
    return jax.shard_map(
        local,
        mesh=mesh,
        in_specs=(
            P("req", None, "exp"),
            P("req", None, None, "exp"),
            P("req", None, None, "exp"),
            P("req"),
            P("exp", None),
            P(("req", "exp"), None),
            P(),
            P(("req", "exp"), None),
            P(("req", "exp"), None),
            P(None, None, ("req", "exp")),
            P(("req", "exp"), None),
        ),
        out_specs=(P(("req", "exp"), None), P(("req", "exp"), None)),
        check_vma=False,
    )
```

```python
import jax
import jax.numpy as jnp
from jax import lax
from jax.sharding import PartitionSpec as P

HD = 128
EXPERTS = 64
FF = 1024
TOP = 8


def local(
    queries,
    new_entries,
    cache_entries,
    cache_lengths,
    out_proj,
    residual,
    norm_gain,
    routes,
    gate_weights,
    expert_in,
    expert_down,
):
    req_local, new_len, width_local = queries.shape
    heads_local = width_local // HD
    cache_len = cache_entries.shape[2]
    tok_local = residual.shape[0]
    model_width = residual.shape[1]

    full_proj = lax.all_gather(out_proj, "exp", axis=0, tiled=True)

    def attend_request(packed):
        query_rows, new_rows, cache_rows, length = packed
        query_heads = query_rows.reshape(new_len, heads_local, HD)
        cache_keys = cache_rows[0].reshape(cache_len, heads_local, HD)
        cache_vals = cache_rows[1].reshape(cache_len, heads_local, HD)
        new_keys = new_rows[0].reshape(new_len, heads_local, HD)
        new_vals = new_rows[1].reshape(new_len, heads_local, HD)
        scale = HD ** (-0.5)
        cache_scores = (
            jnp.einsum("thd,jhd->htj", query_heads, cache_keys, preferred_element_type=jnp.float32)
            * scale
        )
        new_scores = (
            jnp.einsum("thd,jhd->htj", query_heads, new_keys, preferred_element_type=jnp.float32)
            * scale
        )
        cache_valid = jnp.arange(cache_len, dtype=jnp.int32) < length
        causal = (
            jnp.arange(new_len, dtype=jnp.int32)[None, :]
            <= jnp.arange(new_len, dtype=jnp.int32)[:, None]
        )
        scores = jnp.concatenate(
            [
                jnp.where(cache_valid[None, None, :], cache_scores, -1e30),
                jnp.where(causal[None, :, :], new_scores, -1e30),
            ],
            axis=-1,
        )
        peak = jnp.max(scores, axis=-1, keepdims=True)
        weights = jnp.exp(scores - peak)
        denoms = jnp.sum(weights, axis=-1)
        weights_bf = weights.astype(jnp.bfloat16)
        all_vals = jnp.concatenate([cache_vals, new_vals], axis=0)
        mixed = jnp.einsum("htj,jhd->thd", weights_bf, all_vals, preferred_element_type=jnp.float32)
        mixed = mixed / jnp.transpose(denoms)[:, :, None]
        return mixed.astype(jnp.bfloat16).reshape(new_len, width_local)

    attention = lax.map(attend_request, (queries, new_entries, cache_entries, cache_lengths))
    attention = attention.reshape(req_local * new_len, width_local)
    features = lax.all_to_all(attention, "exp", split_axis=0, concat_axis=1, tiled=True)
    projected = jnp.dot(features, full_proj, preferred_element_type=jnp.float32)
    hidden = residual.astype(jnp.float32) + projected
    attended = hidden.astype(jnp.bfloat16)
    mean_square = jnp.mean(hidden * hidden, axis=-1, keepdims=True)
    normed = (hidden * lax.rsqrt(mean_square + 1e-05) * norm_gain).astype(jnp.bfloat16)
    devices = lax.axis_size("req") * lax.axis_size("exp")
    width_units = expert_in.shape[2]
    copies = max(1, FF // width_units)
    experts_local = max(1, width_units // FF)
    capacity = max(2, tok_local * TOP * 5 // (EXPERTS * 4))
    onehot = routes[:, :, None] == jnp.arange(EXPERTS, dtype=jnp.int32)[None, None, :]
    chosen = jnp.any(onehot, axis=1).astype(jnp.bfloat16)
    token_ids = jnp.arange(tok_local, dtype=jnp.int32)
    earlier = (token_ids[None, :] < token_ids[:, None]).astype(jnp.bfloat16)
    rank = jnp.dot(earlier, chosen, preferred_element_type=jnp.float32).astype(jnp.int32)
    slot_index = jnp.sum(jnp.where(onehot, rank[:, None, :], 0), axis=2)
    positions = routes * capacity + slot_index
    places = jnp.transpose(positions)
    items = experts_local * capacity
    cut = items * 3 // 5 // 8 * 8
    bounds = [(0, cut), (cut, items)] if cut else [(0, items)]

    def keys_of(lower, upper):
        count = upper - lower
        index = jnp.arange(devices * count, dtype=jnp.int32)
        slot_ids = index // count * items + lower + index % count
        return slot_ids // (copies * capacity) * capacity + slot_ids % capacity

    def exchange(block, count):
        return lax.all_to_all(
            block.reshape(devices, count, model_width),
            ("req", "exp"),
            split_axis=0,
            concat_axis=0,
            tiled=True,
        ).reshape(devices * count, model_width)

    arrived = []
    for lower, upper in bounds:
        slot_keys = keys_of(lower, upper)
        fill = slot_keys[:, None] == places[0][None, :]
        for choice in range(1, TOP):
            fill = fill | (slot_keys[:, None] == places[choice][None, :])
        outgoing = jnp.dot(
            fill.astype(jnp.bfloat16), normed, preferred_element_type=jnp.float32
        ).astype(jnp.bfloat16)
        arrived.append(exchange(outgoing, upper - lower))
    returned = []
    for (lower, upper), rows in zip(bounds, arrived):
        count = upper - lower
        begin = lower // capacity * FF
        end = min(width_units, ((upper - 1) // capacity + 1) * FF)
        gate_part = jnp.dot(rows, expert_in[0, :, begin:end], preferred_element_type=jnp.float32)
        up_part = jnp.dot(rows, expert_in[1, :, begin:end], preferred_element_type=jnp.float32)
        inner = jax.nn.silu(gate_part) * up_part
        if end - begin > FF:
            row_ids = jnp.arange(devices * count, dtype=jnp.int32)
            row_expert = (row_ids % count + lower) // capacity
            unit_expert = jnp.arange(begin, end, dtype=jnp.int32) // FF
            inner = jnp.where(row_expert[:, None] == unit_expert[None, :], inner, 0.0)
        outputs = jnp.dot(
            inner.astype(jnp.bfloat16), expert_down[begin:end], preferred_element_type=jnp.float32
        ).astype(jnp.bfloat16)
        returned.append(exchange(outputs, count))
    total = jnp.zeros((tok_local, model_width), jnp.float32)
    for (lower, upper), rows in zip(bounds, returned):
        slot_keys = keys_of(lower, upper)
        mix = jnp.zeros((tok_local, slot_keys.shape[0]), jnp.float32)
        for choice in range(TOP):
            mix = mix + jnp.where(
                positions[:, choice][:, None] == slot_keys[None, :],
                gate_weights[:, choice][:, None],
                0.0,
            )
        first = lax.reduce_precision(mix, 8, 7)
        second = lax.reduce_precision(mix - first, 8, 7)
        third = mix - first - second
        terms = jnp.concatenate([first, second, third], axis=0).astype(jnp.bfloat16)
        mixed = jnp.dot(terms, rows, preferred_element_type=jnp.float32)
        mixed = mixed.reshape(3, tok_local, model_width)
        total = total + (mixed[0] + mixed[1] + mixed[2])
    expert_out = total.astype(jnp.bfloat16)
    return (attended, expert_out)


def solution(mesh):
    return jax.shard_map(
        local,
        mesh=mesh,
        in_specs=(
            P("req", None, "exp"),
            P("req", None, None, "exp"),
            P("req", None, None, "exp"),
            P("req"),
            P("exp", None),
            P(("req", "exp"), None),
            P(),
            P(("req", "exp"), None),
            P(("req", "exp"), None),
            P(None, None, ("req", "exp")),
            P(("req", "exp"), None),
        ),
        out_specs=(P(("req", "exp"), None), P(("req", "exp"), None)),
        check_vma=False,
    )
```
